512 devices in a mesh: space: 64 (over z, y), term: 8 (over x, core).
Axes of the slice: x: 4, y: 8, z: 8, core: 2. Of those that a mesh axis runs over, the one named last changes fastest.
Arguments:
- x_modes: bfloat16 [64, 512], P('space'), may hold values from -0.125 to 0.125
- y_modes: bfloat16 [32, 512], replicated, may hold values from -5 to 5
- z_modes: bfloat16 [512, 128], replicated, may hold values from -5 to 5
- coefficients: float32 [64, 512], P('term'), may hold values from -5 to 5
- magic_cells: int32 [32], replicated, may hold values from 0 to 262143
- interp_inverse: float32 [32, 32], replicated, may hold values from -1 to 1, as said below
- eim_basis: bfloat16 [32, 262144], P('term', 'space'), may hold values from 0.006225586 to 0.0625
- basis: bfloat16 [96, 262144], P(None, 'space'), may hold values from -0.013621858 to 0.013621858
Outputs:
- eim_coefficients: float32 [32, 64], P(None, 'term')
- interp_error: bfloat16 [64, 262144], P('term', 'space')
- term_operators: float32 [32, 9216], P('term', 'space')
- assembled: float32 [64, 9216], P('term', 'space')
The draws below stay inside these ranges and needn't reach their ends.
Inputs may be any that keep to these rules, and one draw needn't show every extreme that they name: `interp_inverse`: lower triangular with ones on the diagonal.
All inputs are finite; a program needn't handle non-finite values.
Results may differ from the reference program's by a relative error of at most 0.0015.
The reference program's roundings to bfloat16 on the way count: a program that leaves them out, or rounds other values in their place, can miss the bound.
Values may be sent and summed in bfloat16 or wider, within the bound.
No kernel may reach another device: no remote copies, remote signals or barrier semaphores. Data moves between devices by JAX's collectives and lax.ppermute only.
A program may use at most 64 MiB of HBM per device.

```python
import jax
import jax.numpy as jnp
from jax import lax

M = 512
R = 96
Q = 32
PX = 1
NY = 32
NZ = 128
NX = 64
CELLS = 262144
S = 64
N_SPACE = 64


def draw_interp_inverse(key, part):
    key = jax.random.fold_in(key, 11)
    row_ids = lax.broadcasted_iota(jnp.int32, (Q, Q), 0)
    col_ids = lax.broadcasted_iota(jnp.int32, (Q, Q), 1)
    raw = jnp.clip(jax.random.normal(key, (Q, Q), jnp.float32), -4.0, 4.0)
    lower = jnp.where(col_ids < row_ids, raw * (0.6 * Q ** (-0.5)), 0.0)
    return lower + jnp.where(col_ids == row_ids, 1.0, 0.0)


def draw_basis(key, part):
    key = jax.random.fold_in(key, 23)
    key_own, key_shared, key_gain = jax.random.split(key, 3)
    own = jnp.clip(jax.random.normal(key_own, (R, CELLS), jnp.float32), -5.0, 5.0)
    shared = jnp.clip(jax.random.normal(key_shared, (CELLS,), jnp.float32), -5.0, 5.0)
    gains = jax.random.uniform(key_gain, (R,), jnp.float32, 0.5, 1.5)
    combined = jnp.clip(own + 0.5 * gains[:, None] * shared[None, :], -3.0, 3.0)
    plane_ids = lax.broadcasted_iota(jnp.int32, (CELLS,), 0) // (NY * NZ)
    signs = jnp.where(plane_ids % 2 == 0, 1.0, -1.0).astype(jnp.float32)
    return (combined * signs[None, :] * (6.0 * CELLS / Q) ** (-0.5)).astype(jnp.bfloat16)


def set_ends(entries, rng, least, top_value):
    longest = entries.shape.index(max(entries.shape))
    spots = []
    for shift in (0, 1):
        where = [jax.random.randint(jax.random.fold_in(rng, axis), (), 0, length) for axis, length in enumerate(entries.shape)]
        where[longest] = (where[longest] + shift) % entries.shape[longest]
        spots.append(tuple(where))
    return entries.at[spots[0]].set(least).at[spots[1]].set(top_value)


def shard_levels(rng, shape, shards, low, largest):
    gain, own = 1.0, jax.random.fold_in(rng, 6)
    for axis_at, parts in shards:
        steps = jnp.exp(jax.random.uniform(jax.random.fold_in(own, axis_at), (parts,), jnp.float32, low / len(shards), largest / len(shards)))
        gain = gain * jnp.repeat(steps, shape[axis_at] // parts).reshape([-1 if axis == axis_at else 1 for axis in range(len(shape))])
    return gain


def noise(key, dims, spread, bound, cuts=(), kind=jnp.bfloat16):
    result = jax.random.normal(key, dims, jnp.float32) * spread
    if len(cuts) > 0:
        result = shard_levels(key, dims, cuts, -0.22, 0.18) * result
    return jnp.clip(result, min=-bound, max=bound).astype(kind)


def setup_inputs(seed: int = 0) -> dict:
    splits = jax.random.split(jax.random.key(seed), 9)
    x_modes = noise(splits[0], (NX, M), (4 * M) ** -0.5, 0.125, ((0, 64),))
    y_modes = noise(splits[1], (NY, M), 1.0, 5.0)
    z_modes = noise(splits[2], (M, NZ), 1.0, 5.0)
    coefficients = noise(splits[3], (S, M), 1.0, 5.0, ((0, 8),), jnp.float32)
    magic_cells = set_ends(jax.random.randint(splits[4], (Q,), 0, CELLS), jax.random.fold_in(splits[4], 1), 0, CELLS - 1).astype(jnp.int32)
    interp_inverse = draw_interp_inverse(jax.random.fold_in(splits[8], 71), 0)
    eim_basis = jnp.clip(0.006225586 + 0.056274414 * jax.random.uniform(splits[6], (Q, CELLS), jnp.float32) ** shard_levels(splits[6], (Q, CELLS), ((0, 8), (1, 64)), -0.2, 0.2), 0.006225586, 0.0625).astype(jnp.bfloat16)
    basis = draw_basis(jax.random.fold_in(splits[8], 71), 0)
    return {"x_modes": x_modes, "y_modes": y_modes, "z_modes": z_modes, "coefficients": coefficients, "magic_cells": magic_cells, "interp_inverse": interp_inverse, "eim_basis": eim_basis, "basis": basis}


def log_values(x_rows, y_modes, z_modes, coefficients):
    scaled = x_rows.astype(jnp.float32)[None, :, None, :] * coefficients[:, None, None, :]
    left_factor = (scaled * y_modes.astype(jnp.float32)[None, None, :, :]).astype(jnp.bfloat16)
    snap_count = coefficients.shape[0]
    flattened = left_factor.reshape(-1, left_factor.shape[-1])
    return jnp.dot(flattened, z_modes, preferred_element_type=jnp.float32).reshape(snap_count, -1)


def differences(stacked):
    widened = stacked.astype(jnp.float32)
    current = widened[:, :-1]
    along_x = widened[:, 1:] - current
    zeros_y = jnp.zeros_like(current[:, :, :1])
    along_y = jnp.concatenate([current[:, :, 1:], zeros_y], 2) - current
    zeros_z = jnp.zeros_like(current[:, :, :, :1])
    along_z = jnp.concatenate([current[:, :, :, 1:], zeros_z], 3) - current
    row_count = current.shape[0]
    return [part_diff.astype(jnp.bfloat16).reshape(row_count, -1) for part_diff in (along_x, along_y, along_z)]


def weighted_gram(diff_list, weights):
    summed = None
    for difference in diff_list:
        weighted = (weights.astype(jnp.float32)[:, None, :] * difference.astype(jnp.float32)[None]).astype(jnp.bfloat16)
        weighted = weighted.reshape(-1, difference.shape[1])
        product = lax.dot_general(difference, weighted, (((1,), (1,)), ((), ())), preferred_element_type=jnp.float32)
        summed = product if summed is None else summed + product
    return summed


def reference(x_modes, y_modes, z_modes, coefficients, magic_cells, interp_inverse, eim_basis, basis):
    conductivity = jnp.exp(log_values(x_modes, y_modes, z_modes, coefficients))
    samples = jnp.take(conductivity, magic_cells, axis=1)
    eim_coefficients = jnp.dot(interp_inverse, samples.T, precision=lax.Precision.HIGHEST)
    rounded = eim_coefficients.astype(jnp.bfloat16)
    fitted = lax.dot_general(rounded, eim_basis, (((0,), (0,)), ((), ())), preferred_element_type=jnp.float32)
    interp_error = (conductivity - fitted).astype(jnp.bfloat16)
    basis_grid = basis.reshape(R, NX, NY, NZ)
    padded = jnp.concatenate([basis_grid, jnp.zeros((R, 1, NY, NZ), basis_grid.dtype)], 1)

    def slab_step(summed, slab_index):
        first_plane = (slab_index * PX).astype(jnp.int32)
        slab_block = lax.dynamic_slice_in_dim(padded, first_plane, PX + 1, 1)
        weights = lax.dynamic_slice_in_dim(eim_basis, (first_plane * (NY * NZ)).astype(jnp.int32), PX * NY * NZ, 1)
        return summed + weighted_gram(differences(slab_block), weights), None

    summed, unused = lax.scan(slab_step, jnp.zeros((R, Q * R), jnp.float32), jnp.arange(N_SPACE, dtype=jnp.int32))
    term_operators = summed.reshape(R, Q, R).transpose(1, 0, 2).reshape(Q, R * R)
    assembled = jnp.dot(eim_coefficients.T, term_operators, precision=lax.Precision.HIGHEST)
    return eim_coefficients, interp_error, term_operators, assembled
```

```python
import jax
import jax.numpy as jnp
from jax import lax
from jax.experimental import pallas as pl
from jax.experimental.pallas import tpu as pltpu
from jax.sharding import PartitionSpec as P

F32, BF16 = jnp.float32, jnp.bfloat16
VMEM = pl.BlockSpec(memory_space=pltpu.VMEM)
SMEM = pl.BlockSpec(memory_space=pltpu.SMEM)
CHUNK = 512
EXACT = lax.Precision.HIGHEST


def call(body, out_shape, inputs, specs=None, scratch=(), flops=0, moved=0):
    return pl.pallas_call(
        body,
        out_shape=out_shape,
        in_specs=specs or [VMEM] * len(inputs),
        out_specs=jax.tree.map(lambda _: VMEM, out_shape),
        scratch_shapes=list(scratch),
        compiler_params=pltpu.CompilerParams(vmem_limit_bytes=32 << 20),
        cost_estimate=pl.CostEstimate(flops=flops, bytes_accessed=moved, transcendentals=0),
    )(*inputs)


def gram_of(diff, weights):
    rank, cells = diff.shape
    blocks = diff.reshape(rank // 16, 16, cells)
    weighted = []
    for q in range(weights.shape[0]):
        row = jnp.broadcast_to(weights[q : q + 1], (16, cells)).astype(BF16)
        weighted.append((blocks * row[None]).reshape(rank, cells))
    half = rank // 2
    ordered = [w[:half] for w in weighted] + [w[half:] for w in weighted]
    return lax.dot_general(
        jnp.concatenate(ordered, 0), diff, (((1,), (1,)), ((), ())), preferred_element_type=F32
    )


def inner_gram(width_z, basis_ref, eim_ref, out_ref):
    rank, cells = basis_ref.shape
    last = lax.broadcasted_iota(jnp.int32, (rank, width_z), 1) == width_z - 1
    total = jnp.zeros(out_ref.shape, F32)
    for start in range(0, cells, CHUNK):
        current = basis_ref[:, start : start + CHUNK].astype(F32)
        if start + CHUNK < cells:
            after = basis_ref[:, start + width_z : start + CHUNK + width_z].astype(F32)
        else:
            after = jnp.concatenate([current[:, width_z:], jnp.zeros((rank, width_z), F32)], 1)
        weights = eim_ref[:, start : start + CHUNK].astype(F32)
        total += gram_of((after - current).astype(BF16), weights)
        pieces = []
        for at in range(0, CHUNK, width_z):
            piece = current[:, at : at + width_z]
            moved = jnp.where(last, 0.0, pltpu.roll(piece, width_z - 1, 1))
            pieces.append((moved - piece).astype(BF16))
        total += gram_of(jnp.concatenate(pieces, 1), weights)
    out_ref[...] = total


def own_half(side_ref, basis_ref, out_ref):
    del side_ref
    out_ref[...] = basis_ref[...]


def outer_gram(ranks, side_ref, basis_ref, following_ref, eim_ref, inner_ref, x_ref, out_ref):
    half = following_ref.shape[1]
    depth = inner_ref.shape[0] // 2
    total = []
    for at in (0, depth):
        own = inner_ref[at : at + depth]
        total += [jnp.where(side_ref[0] == 0, own, 0.0), jnp.where(side_ref[0] == 0, 0.0, own)]
    total = jnp.concatenate(total, 0)
    for start in range(0, half, CHUNK):
        part = pl.ds(pl.multiple_of(side_ref[0] * half + start, CHUNK), CHUNK)
        after = following_ref[:, start : start + CHUNK].astype(F32)
        diff = (after - basis_ref[:, part].astype(F32)).astype(BF16)
        total += gram_of(diff, eim_ref[:, part].astype(F32))
    rows = total.T
    width = rows.shape[1]
    modes = x_ref[...].astype(F32)
    fill = jnp.zeros((1, out_ref.shape[2] - width), F32)
    for place, share in enumerate(ranks):
        at = 3 * (share // 2)
        if share % 2 == 0:
            whole, part = rows[at : at + 1], rows[at + 1 : at + 2, : width // 2]
        else:
            whole, part = rows[at + 2 : at + 3], rows[at + 1 : at + 2, width // 2 :]
        whole = jnp.concatenate([whole, fill], 1)
        part = jnp.concatenate([part, modes], 1)
        out_ref[place] = jnp.concatenate([whole, part], 0).astype(BF16)


def in_order(odd_ref, own_ref, other_ref, out_ref):
    own, other = own_ref[...].astype(F32), other_ref[...].astype(F32)
    even = odd_ref[0] == 0
    first, second = jnp.where(even, own, other), jnp.where(even, other, own)
    out_ref[...] = jnp.concatenate([first, second], 0).astype(BF16)


def two_cores(core_ref, own_ref, other_ref, out_ref):
    own, other = own_ref[...].astype(F32), other_ref[...].astype(F32)
    even = core_ref[0] == 0
    first, second = jnp.where(even, own, other), jnp.where(even, other, own)
    terms = own.shape[0] // 2
    rows = [first[:terms], second[:terms], first[terms:], second[terms:]]
    out_ref[...] = jnp.concatenate(rows, 0).astype(BF16)


def field(
    cells_ref, x_ref, y_ref, z_ref, coefficients_ref, at_y_ref, at_z_ref, conductivity_ref, pick_z, wide_y
):
    width_y, width_z = y_ref.shape[0], z_ref.shape[1]
    plane = width_y * width_z
    wide_y[...] = y_ref[...].astype(F32)
    lanes = lax.broadcasted_iota(jnp.int32, (1, width_z), 1)
    for q in range(cells_ref.shape[0]):
        cell = cells_ref[q]
        at_y_ref[q : q + 1] = wide_y[pl.ds((cell % plane) // width_z, 1), :]
        pick_z[q : q + 1] = jnp.where(lanes == cell % width_z, 1.0, 0.0)
    at_z_ref[...] = lax.dot_general(
        pick_z[...].astype(BF16), z_ref[...], (((1,), (1,)), ((), ())), preferred_element_type=F32
    )
    scaled = x_ref[...].astype(F32) * coefficients_ref[...]
    left = [(scaled * wide_y[y : y + 1]).astype(BF16) for y in range(width_y)]
    logs = jnp.dot(jnp.concatenate(left, 0), z_ref[...], preferred_element_type=F32)
    conductivity_ref[...] = jnp.exp(logs)


def interpolation(
    meet, plane, cells_ref, chip_ref, arrived_ref, at_y_ref, at_z_ref, conductivity_ref,
    coefficients_ref, inverse_ref, near_eim_ref, far_eim_ref, turned_ref, kept_ref, error_ref, pick_x,
):
    points, modes = pick_x.shape
    slabs = arrived_ref.shape[0]
    snaps = coefficients_ref.shape[0]
    width_z = conductivity_ref.shape[1]
    gram_width = arrived_ref.shape[2] - modes
    for q in range(points):
        slab = (cells_ref[q] // plane + slabs - meet) % slabs
        pick_x[q : q + 1] = arrived_ref[slab][:, gram_width:].astype(F32)[1:2]
    at_x, at_y, at_z = pick_x[...], at_y_ref[...], at_z_ref[...]
    coefficients = coefficients_ref[...]
    lane = lax.broadcasted_iota(jnp.int32, (points, 128), 1)
    logs = jnp.zeros((points, 128), F32)
    for s in range(snaps):
        left = ((at_x * coefficients[s : s + 1]) * at_y).astype(BF16).astype(F32)
        logs += jnp.where(lane == s, jnp.sum(left * at_z, axis=1, keepdims=True), 0.0)
    samples = jnp.exp(logs)
    values = jnp.dot(inverse_ref[...], samples, precision=EXACT, preferred_element_type=F32)
    turned = values.T[:snaps]
    turned_ref[...] = turned
    kept_ref[...] = turned
    depth = near_eim_ref.shape[0]
    swapped = jnp.concatenate([turned[:, depth:], turned[:, :depth]], 1)
    rounded = jnp.where(chip_ref[0] // 2 == 0, turned, swapped).astype(BF16)
    basis = jnp.concatenate([near_eim_ref[...], far_eim_ref[...]], 0)
    fitted = jnp.dot(rounded, basis, preferred_element_type=F32)
    for y in range(plane // width_z):
        part = slice(y * width_z, (y + 1) * width_z)
        error = conductivity_ref[y * snaps : (y + 1) * snaps] - fitted[:, part]
        error_ref[:, part] = error.astype(BF16)


def own_share(rank, odd_ref, arrived_ref, spread_ref):
    terms = spread_ref.shape[1]
    width = terms * rank
    half = rank // 2
    total = jnp.sum(arrived_ref[:, :, :width].astype(F32), axis=0)
    whole, part = total[0:1], total[1:2, : width // 2]
    odd = odd_ref[0] == 1
    picked = []
    for q in range(terms):
        first = whole[:, q * half : (q + 1) * half]
        second = whole[:, width // 2 + q * half : width // 2 + (q + 1) * half]
        single = part[:, q * half : (q + 1) * half]
        even_form = jnp.concatenate([first, second, single], 1)
        odd_form = jnp.concatenate([single, first, second], 1)
        picked.append(jnp.where(odd, odd_form, even_form))
    own = jnp.concatenate(picked, 0)
    for t in range(spread_ref.shape[0]):
        spread_ref[t] = own


def assembly(turn, core_ref, chip_ref, turned_ref, operators_ref, own_ref, out_ref):
    turned = turned_ref[...]
    count, both = operators_ref.shape[:2]
    terms = both // 2
    total = jnp.zeros(out_ref.shape, F32)
    for first in (0, 1, 4, 5):
        at = (first + count - turn) % count
        block = operators_ref[at] + operators_ref[at + 2]
        for j in range(both):
            q = (first + 2 * (j // terms)) * terms + j % terms
            total += turned[:, q : q + 1] * block[j : j + 1]
    out_ref[...] = total
    at = (4 * (chip_ref[0] // 2) + core_ref[0] + count - turn) % count
    own = operators_ref[at] + operators_ref[at + 2]
    own_ref[...] = jnp.where(chip_ref[0] % 2 == 0, own[:terms], own[terms:])


def local(x_modes, y_modes, z_modes, coefficients, magic_cells, interp_inverse, eim_basis, basis):
    space, term = "space", "term"
    slabs, groups = lax.axis_size(space), lax.axis_size(term)
    modes = x_modes.shape[1]
    width_y, width_z = y_modes.shape[0], z_modes.shape[1]
    snaps, points = coefficients.shape[0], magic_cells.shape[0]
    rank, cells = basis.shape
    terms = eim_basis.shape[0]
    share = rank * rank // slabs
    shape = jax.ShapeDtypeStruct

    slab = lax.axis_index(space).astype(jnp.int32).reshape(1)
    place = lax.axis_index(term).astype(jnp.int32).reshape(1)
    core, chip = place % 2, place // 2
    side = chip % 2
    half = cells // 2
    meet, turn = slabs // 2 + slabs // 16, groups // 2
    ranks = [(meet + i) % slabs for i in range(slabs)]
    term_ranks = [(turn + i) % groups for i in range(groups)]
    swap = [(i, i ^ 1) for i in range(groups)]
    mine = pl.pallas_call(
        own_half,
        out_shape=shape((rank, half), BF16),
        grid_spec=pltpu.PrefetchScalarGridSpec(
            num_scalar_prefetch=1,
            grid=(1,),
            in_specs=[pl.BlockSpec((rank, half), lambda i, side_ref: (0, side_ref[0]))],
            out_specs=pl.BlockSpec((rank, half), lambda i, side_ref: (0, 0)),
        ),
        compiler_params=pltpu.CompilerParams(vmem_limit_bytes=32 << 20),
        cost_estimate=pl.CostEstimate(flops=0, bytes_accessed=2 * basis.size, transcendentals=0),
    )(side, basis)
    near = lax.ppermute(mine, space, [(i + 1, i) for i in range(slabs - 1)])
    eim_beside = lax.ppermute(eim_basis, term, [(i, i ^ 2) for i in range(groups)])
    gram_flops = 2 * rank * rank * terms * cells
    inner = call(
        lambda *refs: inner_gram(width_z, *refs),
        shape((terms * rank, rank), F32),
        (basis, eim_basis),
        flops=2 * gram_flops,
        moved=2 * basis.size,
    )
    eim_beside, inner = lax.optimization_barrier((eim_beside, inner))
    eim_pair = call(
        in_order,
        shape((2 * terms, cells), BF16),
        (side, eim_basis, eim_beside),
        specs=[SMEM, VMEM, VMEM],
        moved=8 * eim_basis.size,
    )
    eim_other = lax.ppermute(eim_pair, term, swap)
    near, inner, eim_pair = lax.optimization_barrier((near, inner, eim_pair))
    packed = call(
        lambda *refs: outer_gram(ranks, *refs),
        shape((slabs, 2, terms * rank + modes), BF16),
        (side, basis, near, eim_pair, inner, x_modes),
        specs=[SMEM] + [VMEM] * 5,
        flops=gram_flops,
        moved=4 * basis.size,
    )
    packed, eim_other, factors = lax.optimization_barrier((packed, eim_other, coefficients))
    eim_near = call(
        two_cores,
        shape((4 * terms, cells), BF16),
        (core, eim_pair, eim_other),
        specs=[SMEM, VMEM, VMEM],
        moved=16 * eim_basis.size,
    )
    eim_far = lax.ppermute(eim_near, term, [(i, i ^ (groups - 2)) for i in range(groups)])
    arrived = lax.all_to_all(packed, space, 0, 0, axis_index_groups=[ranks], tiled=True)
    at_y, at_z, conductivity = call(
        field,
        (
            shape((points, modes), F32),
            shape((points, modes), F32),
            shape((width_y * snaps, width_z), F32),
        ),
        (magic_cells, x_modes, y_modes, z_modes, factors),
        specs=[SMEM] + [VMEM] * 4,
        scratch=[pltpu.VMEM((points, width_z), F32), pltpu.VMEM((width_y, modes), F32)],
        flops=2 * snaps * width_y * modes * width_z,
        moved=4 * points * cells,
    )
    arrived, at_y, at_z, conductivity = lax.optimization_barrier(
        (arrived, at_y, at_z, conductivity)
    )
    eim_turned, turned, interp_error = call(
        lambda *refs: interpolation(meet, cells, *refs),
        (shape((snaps, points), F32), shape((snaps, points), F32), shape((snaps, cells), BF16)),
        (magic_cells, chip, arrived, at_y, at_z, conductivity, coefficients, interp_inverse)
        + (eim_near, eim_far),
        specs=[SMEM] * 2 + [VMEM] * 8,
        scratch=[pltpu.VMEM((points, modes), F32)],
        flops=2 * snaps * points * cells,
        moved=4 * points * cells,
    )
    odd = slab % 2
    spread = call(
        lambda *refs: own_share(rank, *refs),
        shape((groups, 2 * terms, share), F32),
        (odd, arrived),
        specs=[SMEM, VMEM],
        moved=4 * packed.size,
    )
    all_operators = lax.all_to_all(spread, term, 0, 0, axis_index_groups=[term_ranks], tiled=True)
    term_operators, assembled = call(
        lambda *refs: assembly(turn, *refs),
        (shape((terms, share), F32), shape((snaps, share), F32)),
        (core, chip, turned, all_operators),
        specs=[SMEM, SMEM, VMEM, VMEM],
        moved=1 << 15,
    )
    return (eim_turned.T, interp_error, term_operators, assembled)


def solution(mesh):
    space, term = "space", "term"
    placed = (
        P(space, None),
        P(),
        P(),
        P(term, None),
        P(),
        P(),
        P(term, space),
        P(None, space),
    )
    return jax.shard_map(
        local,
        mesh=mesh,
        in_specs=placed,
        out_specs=(P(None, term), P(term, space), P(term, space), P(term, space)),
        check_vma=False,
    )
```

```python
import jax
import jax.numpy as jnp
from jax import lax
from jax.experimental import pallas as pl
from jax.experimental.pallas import tpu as pltpu
from jax.sharding import PartitionSpec as P

F32, BF16 = jnp.float32, jnp.bfloat16
VMEM = pl.BlockSpec(memory_space=pltpu.VMEM)
SMEM = pl.BlockSpec(memory_space=pltpu.SMEM)
CHUNK = 512
EXACT = lax.Precision.HIGHEST


def call(body, out_shape, inputs, specs=None, scratch=(), flops=0, moved=0):
    return pl.pallas_call(
        body,
        out_shape=out_shape,
        in_specs=specs or [VMEM] * len(inputs),
        out_specs=jax.tree.map(lambda _: VMEM, out_shape),
        scratch_shapes=list(scratch),
        compiler_params=pltpu.CompilerParams(vmem_limit_bytes=32 << 20),
        cost_estimate=pl.CostEstimate(flops=flops, bytes_accessed=moved, transcendentals=0),
    )(*inputs)


def gram_of(diff, weights):
    rank, cells = diff.shape
    blocks = diff.reshape(rank // 16, 16, cells)
    weighted = []
    for q in range(weights.shape[0]):
        row = jnp.broadcast_to(weights[q : q + 1], (16, cells)).astype(BF16)
        weighted.append((blocks * row[None]).reshape(rank, cells))
    half = rank // 2
    ordered = [w[:half] for w in weighted] + [w[half:] for w in weighted]
    return lax.dot_general(
        jnp.concatenate(ordered, 0), diff, (((1,), (1,)), ((), ())), preferred_element_type=F32
    )


def inner_gram(width_z, basis_ref, eim_ref, out_ref):
    rank, cells = basis_ref.shape
    last = lax.broadcasted_iota(jnp.int32, (rank, width_z), 1) == width_z - 1
    total = jnp.zeros(out_ref.shape, F32)
    for start in range(0, cells, CHUNK):
        current = basis_ref[:, start : start + CHUNK].astype(F32)
        if start + CHUNK < cells:
            after = basis_ref[:, start + width_z : start + CHUNK + width_z].astype(F32)
        else:
            after = jnp.concatenate([current[:, width_z:], jnp.zeros((rank, width_z), F32)], 1)
        weights = eim_ref[:, start : start + CHUNK].astype(F32)
        total += gram_of((after - current).astype(BF16), weights)
        pieces = []
        for at in range(0, CHUNK, width_z):
            piece = current[:, at : at + width_z]
            moved = jnp.where(last, 0.0, pltpu.roll(piece, width_z - 1, 1))
            pieces.append((moved - piece).astype(BF16))
        total += gram_of(jnp.concatenate(pieces, 1), weights)
    out_ref[...] = total


def own_half(side_ref, basis_ref, out_ref):
    del side_ref
    out_ref[...] = basis_ref[...]


def outer_gram(ranks, side_ref, basis_ref, following_ref, eim_ref, inner_ref, x_ref, y_ref, z_ref, out_ref):
    del y_ref, z_ref
    half = following_ref.shape[1]
    depth = inner_ref.shape[0] // 2
    total = []
    for at in (0, depth):
        own = inner_ref[at : at + depth]
        total += [jnp.where(side_ref[0] == 0, own, 0.0), jnp.where(side_ref[0] == 0, 0.0, own)]
    total = jnp.concatenate(total, 0)
    for start in range(0, half, CHUNK):
        part = pl.ds(pl.multiple_of(side_ref[0] * half + start, CHUNK), CHUNK)
        after = following_ref[:, start : start + CHUNK].astype(F32)
        diff = (after - basis_ref[:, part].astype(F32)).astype(BF16)
        total += gram_of(diff, eim_ref[:, part].astype(F32))
    rows = total.T
    width = rows.shape[1]
    modes = x_ref[...].astype(F32)
    fill = jnp.zeros((1, out_ref.shape[2] - width), F32)
    for place, share in enumerate(ranks):
        at = 3 * (share // 2)
        if share % 2 == 0:
            whole, part = rows[at : at + 1], rows[at + 1 : at + 2, : width // 2]
        else:
            whole, part = rows[at + 2 : at + 3], rows[at + 1 : at + 2, width // 2 :]
        whole = jnp.concatenate([whole, fill], 1)
        part = jnp.concatenate([part, modes], 1)
        out_ref[place] = jnp.concatenate([whole, part], 0).astype(BF16)


def in_order(odd_ref, own_ref, other_ref, out_ref):
    own, other = own_ref[...].astype(F32), other_ref[...].astype(F32)
    even = odd_ref[0] == 0
    first, second = jnp.where(even, own, other), jnp.where(even, other, own)
    out_ref[...] = jnp.concatenate([first, second], 0).astype(BF16)


def two_cores(core_ref, own_ref, other_ref, out_ref):
    own, other = own_ref[...].astype(F32), other_ref[...].astype(F32)
    even = core_ref[0] == 0
    first, second = jnp.where(even, own, other), jnp.where(even, other, own)
    terms = own.shape[0] // 2
    rows = [first[:terms], second[:terms], first[terms:], second[terms:]]
    out_ref[...] = jnp.concatenate(rows, 0).astype(BF16)


def field(
    cells_ref, x_ref, y_ref, z_ref, coefficients_ref, at_y_ref, at_z_ref, conductivity_ref, pick_z, wide_y
):
    width_y, width_z = y_ref.shape[0], z_ref.shape[1]
    plane = width_y * width_z
    wide_y[...] = y_ref[...].astype(F32)
    lanes = lax.broadcasted_iota(jnp.int32, (1, width_z), 1)
    for q in range(cells_ref.shape[0]):
        cell = cells_ref[q]
        at_y_ref[q : q + 1] = wide_y[pl.ds((cell % plane) // width_z, 1), :]
        pick_z[q : q + 1] = jnp.where(lanes == cell % width_z, 1.0, 0.0)
    at_z_ref[...] = lax.dot_general(
        pick_z[...].astype(BF16), z_ref[...], (((1,), (1,)), ((), ())), preferred_element_type=F32
    )
    scaled = x_ref[...].astype(F32) * coefficients_ref[...]
    left = [(scaled * wide_y[y : y + 1]).astype(BF16) for y in range(width_y)]
    logs = jnp.dot(jnp.concatenate(left, 0), z_ref[...], preferred_element_type=F32)
    conductivity_ref[...] = jnp.exp(logs)


def interpolation(
    meet, plane, cells_ref, chip_ref, arrived_ref, at_y_ref, at_z_ref, conductivity_ref,
    coefficients_ref, inverse_ref, near_eim_ref, far_eim_ref, turned_ref, kept_ref, error_ref, pick_x,
):
    points, modes = pick_x.shape
    slabs = arrived_ref.shape[0]
    snaps = coefficients_ref.shape[0]
    width_z = conductivity_ref.shape[1]
    gram_width = arrived_ref.shape[2] - modes
    for q in range(points):
        slab = (cells_ref[q] // plane + slabs - meet) % slabs
        pick_x[q : q + 1] = arrived_ref[slab][:, gram_width:].astype(F32)[1:2]
    at_x, at_y, at_z = pick_x[...], at_y_ref[...], at_z_ref[...]
    coefficients = coefficients_ref[...]
    lane = lax.broadcasted_iota(jnp.int32, (points, 128), 1)
    logs = jnp.zeros((points, 128), F32)
    for s in range(snaps):
        left = ((at_x * coefficients[s : s + 1]) * at_y).astype(BF16).astype(F32)
        logs += jnp.where(lane == s, jnp.sum(left * at_z, axis=1, keepdims=True), 0.0)
    samples = jnp.exp(logs)
    values = jnp.dot(inverse_ref[...], samples, precision=EXACT, preferred_element_type=F32)
    turned = values.T[:snaps]
    turned_ref[...] = turned
    kept_ref[...] = turned
    depth = near_eim_ref.shape[0]
    swapped = jnp.concatenate([turned[:, depth:], turned[:, :depth]], 1)
    rounded = jnp.where(chip_ref[0] // 2 == 0, turned, swapped).astype(BF16)
    basis = jnp.concatenate([near_eim_ref[...], far_eim_ref[...]], 0)
    fitted = jnp.dot(rounded, basis, preferred_element_type=F32)
    for y in range(plane // width_z):
        part = slice(y * width_z, (y + 1) * width_z)
        error = conductivity_ref[y * snaps : (y + 1) * snaps] - fitted[:, part]
        error_ref[:, part] = error.astype(BF16)


def own_share(rank, odd_ref, arrived_ref, spread_ref):
    terms = spread_ref.shape[1]
    width = terms * rank
    half = rank // 2
    total = jnp.sum(arrived_ref[:, :, :width].astype(F32), axis=0)
    whole, part = total[0:1], total[1:2, : width // 2]
    odd = odd_ref[0] == 1
    picked = []
    for q in range(terms):
        first = whole[:, q * half : (q + 1) * half]
        second = whole[:, width // 2 + q * half : width // 2 + (q + 1) * half]
        single = part[:, q * half : (q + 1) * half]
        even_form = jnp.concatenate([first, second, single], 1)
        odd_form = jnp.concatenate([single, first, second], 1)
        picked.append(jnp.where(odd, odd_form, even_form))
    own = jnp.concatenate(picked, 0)
    for t in range(spread_ref.shape[0]):
        spread_ref[t] = own


def assembly(turn, core_ref, chip_ref, turned_ref, operators_ref, own_ref, out_ref):
    turned = turned_ref[...]
    count, both = operators_ref.shape[:2]
    terms = both // 2
    total = jnp.zeros(out_ref.shape, F32)
    for first in (0, 1, 4, 5):
        at = (first + count - turn) % count
        block = operators_ref[at] + operators_ref[at + 2]
        for j in range(both):
            q = (first + 2 * (j // terms)) * terms + j % terms
            total += turned[:, q : q + 1] * block[j : j + 1]
    out_ref[...] = total
    at = (4 * (chip_ref[0] // 2) + core_ref[0] + count - turn) % count
    own = operators_ref[at] + operators_ref[at + 2]
    own_ref[...] = jnp.where(chip_ref[0] % 2 == 0, own[:terms], own[terms:])


def local(x_modes, y_modes, z_modes, coefficients, magic_cells, interp_inverse, eim_basis, basis):
    space, term = "space", "term"
    slabs, groups = lax.axis_size(space), lax.axis_size(term)
    modes = x_modes.shape[1]
    width_y, width_z = y_modes.shape[0], z_modes.shape[1]
    snaps, points = coefficients.shape[0], magic_cells.shape[0]
    rank, cells = basis.shape
    terms = eim_basis.shape[0]
    share = rank * rank // slabs
    shape = jax.ShapeDtypeStruct

    slab = lax.axis_index(space).astype(jnp.int32).reshape(1)
    place = lax.axis_index(term).astype(jnp.int32).reshape(1)
    core, chip = place % 2, place // 2
    side = chip % 2
    half = cells // 2
    meet, turn = slabs // 2 + slabs // 16, groups // 2
    ranks = [(meet + i) % slabs for i in range(slabs)]
    term_ranks = [(turn + i) % groups for i in range(groups)]
    swap = [(i, i ^ 1) for i in range(groups)]
    mine = pl.pallas_call(
        own_half,
        out_shape=shape((rank, half), BF16),
        grid_spec=pltpu.PrefetchScalarGridSpec(
            num_scalar_prefetch=1,
            grid=(1,),
            in_specs=[pl.BlockSpec((rank, half), lambda i, side_ref: (0, side_ref[0]))],
            out_specs=pl.BlockSpec((rank, half), lambda i, side_ref: (0, 0)),
        ),
        compiler_params=pltpu.CompilerParams(vmem_limit_bytes=32 << 20),
        cost_estimate=pl.CostEstimate(flops=0, bytes_accessed=2 * basis.size, transcendentals=0),
    )(side, basis)
    near = lax.ppermute(mine, space, [(i + 1, i) for i in range(slabs - 1)])
    eim_beside = lax.ppermute(eim_basis, term, [(i, i ^ 2) for i in range(groups)])
    gram_flops = 2 * rank * rank * terms * cells
    inner = call(
        lambda *refs: inner_gram(width_z, *refs),
        shape((terms * rank, rank), F32),
        (basis, eim_basis),
        flops=2 * gram_flops,
        moved=2 * basis.size,
    )
    eim_beside, inner = lax.optimization_barrier((eim_beside, inner))
    eim_pair = call(
        in_order,
        shape((2 * terms, cells), BF16),
        (side, eim_basis, eim_beside),
        specs=[SMEM, VMEM, VMEM],
        moved=8 * eim_basis.size,
    )
    eim_other = lax.ppermute(eim_pair, term, swap)
    near, inner, eim_pair = lax.optimization_barrier((near, inner, eim_pair))
    packed = call(
        lambda *refs: outer_gram(ranks, *refs),
        shape((slabs, 2, terms * rank + modes), BF16),
        (side, basis, near, eim_pair, inner, x_modes, y_modes, z_modes),
        specs=[SMEM] + [VMEM] * 7,
        flops=gram_flops,
        moved=4 * basis.size,
    )
    packed, eim_other, factors = lax.optimization_barrier((packed, eim_other, coefficients))
    arrived = lax.all_to_all(packed, space, 0, 0, axis_index_groups=[ranks], tiled=True)
    at_y, at_z, conductivity = call(
        field,
        (
            shape((points, modes), F32),
            shape((points, modes), F32),
            shape((width_y * snaps, width_z), F32),
        ),
        (magic_cells, x_modes, y_modes, z_modes, factors),
        specs=[SMEM] + [VMEM] * 4,
        scratch=[pltpu.VMEM((points, width_z), F32), pltpu.VMEM((width_y, modes), F32)],
        flops=2 * snaps * width_y * modes * width_z,
        moved=4 * points * cells,
    )
    eim_other, at_y, at_z, conductivity = lax.optimization_barrier(
        (eim_other, at_y, at_z, conductivity)
    )
    eim_near = call(
        two_cores,
        shape((4 * terms, cells), BF16),
        (core, eim_pair, eim_other),
        specs=[SMEM, VMEM, VMEM],
        moved=16 * eim_basis.size,
    )
    eim_far = lax.ppermute(eim_near, term, [(i, i ^ (groups - 2)) for i in range(groups)])
    arrived, at_y, at_z, conductivity = lax.optimization_barrier(
        (arrived, at_y, at_z, conductivity)
    )
    eim_turned, turned, interp_error = call(
        lambda *refs: interpolation(meet, cells, *refs),
        (shape((snaps, points), F32), shape((snaps, points), F32), shape((snaps, cells), BF16)),
        (magic_cells, chip, arrived, at_y, at_z, conductivity, coefficients, interp_inverse)
        + (eim_near, eim_far),
        specs=[SMEM] * 2 + [VMEM] * 8,
        scratch=[pltpu.VMEM((points, modes), F32)],
        flops=2 * snaps * points * cells,
        moved=4 * points * cells,
    )
    odd = slab % 2
    spread = call(
        lambda *refs: own_share(rank, *refs),
        shape((groups, 2 * terms, share), F32),
        (odd, arrived),
        specs=[SMEM, VMEM],
        moved=4 * packed.size,
    )
    all_operators = lax.all_to_all(spread, term, 0, 0, axis_index_groups=[term_ranks], tiled=True)
    term_operators, assembled = call(
        lambda *refs: assembly(turn, *refs),
        (shape((terms, share), F32), shape((snaps, share), F32)),
        (core, chip, turned, all_operators),
        specs=[SMEM, SMEM, VMEM, VMEM],
        moved=1 << 15,
    )
    return (eim_turned.T, interp_error, term_operators, assembled)


def solution(mesh):
    space, term = "space", "term"
    placed = (
        P(space, None),
        P(),
        P(),
        P(term, None),
        P(),
        P(),
        P(term, space),
        P(None, space),
    )
    return jax.shard_map(
        local,
        mesh=mesh,
        in_specs=placed,
        out_specs=(P(None, term), P(term, space), P(term, space), P(term, space)),
        check_vma=False,
    )
```

```python
import jax
import jax.numpy as jnp
from jax import lax
from jax.experimental import pallas as pl
from jax.experimental.pallas import tpu as pltpu
from jax.sharding import PartitionSpec as P

F32, BF16 = jnp.float32, jnp.bfloat16
VMEM = pl.BlockSpec(memory_space=pltpu.VMEM)
SMEM = pl.BlockSpec(memory_space=pltpu.SMEM)
CHUNK = 512
EXACT = lax.Precision.HIGHEST


def call(body, out_shape, inputs, specs=None, scratch=(), flops=0, moved=0):
    return pl.pallas_call(
        body,
        out_shape=out_shape,
        in_specs=specs or [VMEM] * len(inputs),
        out_specs=jax.tree.map(lambda _: VMEM, out_shape),
        scratch_shapes=list(scratch),
        compiler_params=pltpu.CompilerParams(vmem_limit_bytes=32 << 20),
        cost_estimate=pl.CostEstimate(flops=flops, bytes_accessed=moved, transcendentals=0),
    )(*inputs)


def gram_of(diff, weights):
    rank, cells = diff.shape
    blocks = diff.reshape(rank // 16, 16, cells)
    weighted = []
    for q in range(weights.shape[0]):
        row = jnp.broadcast_to(weights[q : q + 1], (16, cells)).astype(BF16)
        weighted.append((blocks * row[None]).reshape(rank, cells))
    half = rank // 2
    ordered = [w[:half] for w in weighted] + [w[half:] for w in weighted]
    return lax.dot_general(
        jnp.concatenate(ordered, 0), diff, (((1,), (1,)), ((), ())), preferred_element_type=F32
    )


def inner_gram(width_z, basis_ref, eim_ref, out_ref):
    rank, cells = basis_ref.shape
    last = lax.broadcasted_iota(jnp.int32, (rank, width_z), 1) == width_z - 1
    total = jnp.zeros(out_ref.shape, F32)
    for start in range(0, cells, CHUNK):
        current = basis_ref[:, start : start + CHUNK].astype(F32)
        if start + CHUNK < cells:
            after = basis_ref[:, start + width_z : start + CHUNK + width_z].astype(F32)
        else:
            after = jnp.concatenate([current[:, width_z:], jnp.zeros((rank, width_z), F32)], 1)
        weights = eim_ref[:, start : start + CHUNK].astype(F32)
        total += gram_of((after - current).astype(BF16), weights)
        pieces = []
        for at in range(0, CHUNK, width_z):
            piece = current[:, at : at + width_z]
            moved = jnp.where(last, 0.0, pltpu.roll(piece, width_z - 1, 1))
            pieces.append((moved - piece).astype(BF16))
        total += gram_of(jnp.concatenate(pieces, 1), weights)
    out_ref[...] = total


def own_half(side_ref, basis_ref, out_ref):
    del side_ref
    out_ref[...] = basis_ref[...]


def outer_gram(ranks, side_ref, basis_ref, following_ref, eim_ref, inner_ref, x_ref, out_ref):
    half = following_ref.shape[1]
    depth = inner_ref.shape[0] // 2
    total = []
    for at in (0, depth):
        own = inner_ref[at : at + depth]
        total += [jnp.where(side_ref[0] == 0, own, 0.0), jnp.where(side_ref[0] == 0, 0.0, own)]
    total = jnp.concatenate(total, 0)
    for start in range(0, half, CHUNK):
        part = pl.ds(pl.multiple_of(side_ref[0] * half + start, CHUNK), CHUNK)
        after = following_ref[:, start : start + CHUNK].astype(F32)
        diff = (after - basis_ref[:, part].astype(F32)).astype(BF16)
        total += gram_of(diff, eim_ref[:, part].astype(F32))
    rows = total.T
    width = rows.shape[1]
    modes = x_ref[...].astype(F32)
    fill = jnp.zeros((1, out_ref.shape[2] - width), F32)
    for place, share in enumerate(ranks):
        at = 3 * (share // 2)
        if share % 2 == 0:
            whole, part = rows[at : at + 1], rows[at + 1 : at + 2, : width // 2]
        else:
            whole, part = rows[at + 2 : at + 3], rows[at + 1 : at + 2, width // 2 :]
        whole = jnp.concatenate([whole, fill], 1)
        part = jnp.concatenate([part, modes], 1)
        out_ref[place] = jnp.concatenate([whole, part], 0).astype(BF16)


def in_order(odd_ref, own_ref, other_ref, out_ref):
    own, other = own_ref[...].astype(F32), other_ref[...].astype(F32)
    even = odd_ref[0] == 0
    first, second = jnp.where(even, own, other), jnp.where(even, other, own)
    out_ref[...] = jnp.concatenate([first, second], 0).astype(BF16)


def field(
    cells_ref, x_ref, y_ref, z_ref, coefficients_ref, at_y_ref, at_z_ref, conductivity_ref, pick_z, wide_y
):
    width_y, width_z = y_ref.shape[0], z_ref.shape[1]
    plane = width_y * width_z
    wide_y[...] = y_ref[...].astype(F32)
    lanes = lax.broadcasted_iota(jnp.int32, (1, width_z), 1)
    for q in range(cells_ref.shape[0]):
        cell = cells_ref[q]
        at_y_ref[q : q + 1] = wide_y[pl.ds((cell % plane) // width_z, 1), :]
        pick_z[q : q + 1] = jnp.where(lanes == cell % width_z, 1.0, 0.0)
    at_z_ref[...] = lax.dot_general(
        pick_z[...].astype(BF16), z_ref[...], (((1,), (1,)), ((), ())), preferred_element_type=F32
    )
    scaled = x_ref[...].astype(F32) * coefficients_ref[...]
    left = [(scaled * wide_y[y : y + 1]).astype(BF16) for y in range(width_y)]
    logs = jnp.dot(jnp.concatenate(left, 0), z_ref[...], preferred_element_type=F32)
    conductivity_ref[...] = jnp.exp(logs)


def interpolation(
    meet, plane, cells_ref, chip_ref, arrived_ref, at_y_ref, at_z_ref, conductivity_ref,
    coefficients_ref, inverse_ref, near_eim_ref, far_eim_ref, turned_ref, kept_ref, error_ref, pick_x,
):
    points, modes = pick_x.shape
    slabs = arrived_ref.shape[0]
    snaps = coefficients_ref.shape[0]
    width_z = conductivity_ref.shape[1]
    gram_width = arrived_ref.shape[2] - modes
    for q in range(points):
        slab = (cells_ref[q] // plane + slabs - meet) % slabs
        pick_x[q : q + 1] = arrived_ref[slab][:, gram_width:].astype(F32)[1:2]
    at_x, at_y, at_z = pick_x[...], at_y_ref[...], at_z_ref[...]
    coefficients = coefficients_ref[...]
    lane = lax.broadcasted_iota(jnp.int32, (points, 128), 1)
    logs = jnp.zeros((points, 128), F32)
    for s in range(snaps):
        left = ((at_x * coefficients[s : s + 1]) * at_y).astype(BF16).astype(F32)
        logs += jnp.where(lane == s, jnp.sum(left * at_z, axis=1, keepdims=True), 0.0)
    samples = jnp.exp(logs)
    values = jnp.dot(inverse_ref[...], samples, precision=EXACT, preferred_element_type=F32)
    turned = values.T[:snaps]
    turned_ref[...] = turned
    kept_ref[...] = turned
    depth = near_eim_ref.shape[0]
    swapped = jnp.concatenate([turned[:, depth:], turned[:, :depth]], 1)
    rounded = jnp.where(chip_ref[0] // 2 == 0, turned, swapped).astype(BF16)
    basis = jnp.concatenate([near_eim_ref[...], far_eim_ref[...]], 0)
    fitted = jnp.dot(rounded, basis, preferred_element_type=F32)
    for y in range(plane // width_z):
        part = slice(y * width_z, (y + 1) * width_z)
        error = conductivity_ref[y * snaps : (y + 1) * snaps] - fitted[:, part]
        error_ref[:, part] = error.astype(BF16)


def own_share(rank, odd_ref, arrived_ref, spread_ref):
    terms = spread_ref.shape[1]
    width = terms * rank
    half = rank // 2
    total = jnp.sum(arrived_ref[:, :, :width].astype(F32), axis=0)
    whole, part = total[0:1], total[1:2, : width // 2]
    odd = odd_ref[0] == 1
    picked = []
    for q in range(terms):
        first = whole[:, q * half : (q + 1) * half]
        second = whole[:, width // 2 + q * half : width // 2 + (q + 1) * half]
        single = part[:, q * half : (q + 1) * half]
        even_form = jnp.concatenate([first, second, single], 1)
        odd_form = jnp.concatenate([single, first, second], 1)
        picked.append(jnp.where(odd, odd_form, even_form))
    own = jnp.concatenate(picked, 0)
    for t in range(spread_ref.shape[0]):
        spread_ref[t] = own


def assembly(turn, core_ref, chip_ref, turned_ref, operators_ref, own_ref, out_ref):
    turned = turned_ref[...]
    count, terms = operators_ref.shape[:2]
    total = jnp.zeros(out_ref.shape, F32)
    for chip in range(count // 2):
        at = (2 * chip + count - turn) % count
        block = operators_ref[at] + operators_ref[at + 1]
        for j in range(terms):
            q = chip * terms + j
            total += turned[:, q : q + 1] * block[j : j + 1]
    out_ref[...] = total
    at = (2 * chip_ref[0] + count - turn) % count
    own = operators_ref[at] + operators_ref[at + 1]
    own_ref[...] = jnp.where(core_ref[0] == 0, own[: terms // 2], own[terms // 2 :])


def local(x_modes, y_modes, z_modes, coefficients, magic_cells, interp_inverse, eim_basis, basis):
    space, term = "space", "term"
    slabs, groups = lax.axis_size(space), lax.axis_size(term)
    modes = x_modes.shape[1]
    width_y, width_z = y_modes.shape[0], z_modes.shape[1]
    snaps, points = coefficients.shape[0], magic_cells.shape[0]
    rank, cells = basis.shape
    terms = eim_basis.shape[0]
    share = rank * rank // slabs
    shape = jax.ShapeDtypeStruct

    slab = lax.axis_index(space).astype(jnp.int32).reshape(1)
    place = lax.axis_index(term).astype(jnp.int32).reshape(1)
    core, chip = place % 2, place // 2
    side = chip % 2
    half = cells // 2
    meet, turn = slabs // 2 + slabs // 16, groups // 2
    ranks = [(meet + i) % slabs for i in range(slabs)]
    term_ranks = [(turn + i) % groups for i in range(groups)]
    swap = [(i, i ^ 1) for i in range(groups)]
    mine = pl.pallas_call(
        own_half,
        out_shape=shape((rank, half), BF16),
        grid_spec=pltpu.PrefetchScalarGridSpec(
            num_scalar_prefetch=1,
            grid=(1,),
            in_specs=[pl.BlockSpec((rank, half), lambda i, side_ref: (0, side_ref[0]))],
            out_specs=pl.BlockSpec((rank, half), lambda i, side_ref: (0, 0)),
        ),
        compiler_params=pltpu.CompilerParams(vmem_limit_bytes=32 << 20),
        cost_estimate=pl.CostEstimate(flops=0, bytes_accessed=2 * basis.size, transcendentals=0),
    )(core, basis)
    near = lax.ppermute(mine, space, [(i + 1, i) for i in range(slabs - 1)])
    eim_other = lax.ppermute(eim_basis, term, swap)
    gram_flops = 2 * rank * rank * terms * cells
    inner = call(
        lambda *refs: inner_gram(width_z, *refs),
        shape((terms * rank, rank), F32),
        (basis, eim_basis),
        flops=2 * gram_flops,
        moved=2 * basis.size,
    )
    eim_other, inner = lax.optimization_barrier((eim_other, inner))
    eim_pair = call(
        in_order,
        shape((2 * terms, cells), BF16),
        (core, eim_basis, eim_other),
        specs=[SMEM, VMEM, VMEM],
        moved=8 * eim_basis.size,
    )
    eim_beside = lax.ppermute(eim_pair, term, [(i, i ^ 2) for i in range(groups)])
    near, inner, eim_pair = lax.optimization_barrier((near, inner, eim_pair))
    packed = call(
        lambda *refs: outer_gram(ranks, *refs),
        shape((slabs, 2, terms * rank + modes), BF16),
        (core, basis, near, eim_pair, inner, x_modes),
        specs=[SMEM] + [VMEM] * 5,
        flops=gram_flops,
        moved=4 * basis.size,
    )
    packed, eim_beside, factors = lax.optimization_barrier((packed, eim_beside, coefficients))
    eim_near = call(
        in_order,
        shape((4 * terms, cells), BF16),
        (side, eim_pair, eim_beside),
        specs=[SMEM, VMEM, VMEM],
        moved=16 * eim_basis.size,
    )
    eim_far = lax.ppermute(eim_near, term, [(i, i ^ (groups - 2)) for i in range(groups)])
    arrived = lax.all_to_all(packed, space, 0, 0, axis_index_groups=[ranks], tiled=True)
    at_y, at_z, conductivity = call(
        field,
        (
            shape((points, modes), F32),
            shape((points, modes), F32),
            shape((width_y * snaps, width_z), F32),
        ),
        (magic_cells, x_modes, y_modes, z_modes, factors),
        specs=[SMEM] + [VMEM] * 4,
        scratch=[pltpu.VMEM((points, width_z), F32), pltpu.VMEM((width_y, modes), F32)],
        flops=2 * snaps * width_y * modes * width_z,
        moved=4 * points * cells,
    )
    arrived, at_y, at_z, conductivity = lax.optimization_barrier(
        (arrived, at_y, at_z, conductivity)
    )
    eim_turned, turned, interp_error = call(
        lambda *refs: interpolation(meet, cells, *refs),
        (shape((snaps, points), F32), shape((snaps, points), F32), shape((snaps, cells), BF16)),
        (magic_cells, chip, arrived, at_y, at_z, conductivity, coefficients, interp_inverse)
        + (eim_near, eim_far),
        specs=[SMEM] * 2 + [VMEM] * 8,
        scratch=[pltpu.VMEM((points, modes), F32)],
        flops=2 * snaps * points * cells,
        moved=4 * points * cells,
    )
    odd = slab % 2
    spread = call(
        lambda *refs: own_share(rank, *refs),
        shape((groups, 2 * terms, share), F32),
        (odd, arrived),
        specs=[SMEM, VMEM],
        moved=4 * packed.size,
    )
    all_operators = lax.all_to_all(spread, term, 0, 0, axis_index_groups=[term_ranks], tiled=True)
    term_operators, assembled = call(
        lambda *refs: assembly(turn, *refs),
        (shape((terms, share), F32), shape((snaps, share), F32)),
        (core, chip, turned, all_operators),
        specs=[SMEM, SMEM, VMEM, VMEM],
        moved=1 << 15,
    )
    return (eim_turned.T, interp_error, term_operators, assembled)


def solution(mesh):
    space, term = "space", "term"
    placed = (
        P(space, None),
        P(),
        P(),
        P(term, None),
        P(),
        P(),
        P(term, space),
        P(None, space),
    )
    return jax.shard_map(
        local,
        mesh=mesh,
        in_specs=placed,
        out_specs=(P(None, term), P(term, space), P(term, space), P(term, space)),
        check_vma=False,
    )
```

```python
import jax
import jax.numpy as jnp
from jax import lax
from jax.experimental import pallas as pl
from jax.experimental.pallas import tpu as pltpu
from jax.sharding import PartitionSpec as P

F32, BF16 = jnp.float32, jnp.bfloat16
VMEM = pl.BlockSpec(memory_space=pltpu.VMEM)
SMEM = pl.BlockSpec(memory_space=pltpu.SMEM)
CHUNK = 512
EXACT = lax.Precision.HIGHEST


def call(body, out_shape, inputs, specs=None, scratch=(), flops=0, moved=0):
    return pl.pallas_call(
        body,
        out_shape=out_shape,
        in_specs=specs or [VMEM] * len(inputs),
        out_specs=jax.tree.map(lambda _: VMEM, out_shape),
        scratch_shapes=list(scratch),
        compiler_params=pltpu.CompilerParams(vmem_limit_bytes=32 << 20),
        cost_estimate=pl.CostEstimate(flops=flops, bytes_accessed=moved, transcendentals=0),
    )(*inputs)


def gram_of(diff, weights):
    rank, cells = diff.shape
    blocks = diff.reshape(rank // 16, 16, cells)
    weighted = []
    for q in range(weights.shape[0]):
        row = jnp.broadcast_to(weights[q : q + 1], (16, cells)).astype(BF16)
        weighted.append((blocks * row[None]).reshape(rank, cells))
    half = rank // 2
    ordered = [w[:half] for w in weighted] + [w[half:] for w in weighted]
    return lax.dot_general(
        jnp.concatenate(ordered, 0), diff, (((1,), (1,)), ((), ())), preferred_element_type=F32
    )


def inner_gram(width_z, basis_ref, eim_ref, out_ref):
    rank, cells = basis_ref.shape
    last = lax.broadcasted_iota(jnp.int32, (rank, width_z), 1) == width_z - 1
    total = jnp.zeros(out_ref.shape, F32)
    for start in range(0, cells, CHUNK):
        current = basis_ref[:, start : start + CHUNK].astype(F32)
        if start + CHUNK < cells:
            after = basis_ref[:, start + width_z : start + CHUNK + width_z].astype(F32)
        else:
            after = jnp.concatenate([current[:, width_z:], jnp.zeros((rank, width_z), F32)], 1)
        weights = eim_ref[:, start : start + CHUNK].astype(F32)
        total += gram_of((after - current).astype(BF16), weights)
        pieces = []
        for at in range(0, CHUNK, width_z):
            piece = current[:, at : at + width_z]
            moved = jnp.where(last, 0.0, pltpu.roll(piece, width_z - 1, 1))
            pieces.append((moved - piece).astype(BF16))
        total += gram_of(jnp.concatenate(pieces, 1), weights)
    out_ref[...] = total


def own_half(side_ref, basis_ref, out_ref):
    del side_ref
    out_ref[...] = basis_ref[...]


def outer_gram(ranks, side_ref, basis_ref, following_ref, eim_ref, inner_ref, x_ref, out_ref):
    half = following_ref.shape[1]
    depth = inner_ref.shape[0] // 2
    total = []
    for at in (0, depth):
        own = inner_ref[at : at + depth]
        total += [jnp.where(side_ref[0] == 0, own, 0.0), jnp.where(side_ref[0] == 0, 0.0, own)]
    total = jnp.concatenate(total, 0)
    for start in range(0, half, CHUNK):
        part = pl.ds(pl.multiple_of(side_ref[0] * half + start, CHUNK), CHUNK)
        after = following_ref[:, start : start + CHUNK].astype(F32)
        diff = (after - basis_ref[:, part].astype(F32)).astype(BF16)
        total += gram_of(diff, eim_ref[:, part].astype(F32))
    rows = total.T
    width = rows.shape[1]
    modes = x_ref[...].astype(F32)
    fill = jnp.zeros((1, out_ref.shape[2] - width), F32)
    for place, share in enumerate(ranks):
        at = 3 * (share // 2)
        if share % 2 == 0:
            whole, part = rows[at : at + 1], rows[at + 1 : at + 2, : width // 2]
        else:
            whole, part = rows[at + 2 : at + 3], rows[at + 1 : at + 2, width // 2 :]
        whole = jnp.concatenate([whole, fill], 1)
        part = jnp.concatenate([part, modes], 1)
        out_ref[place] = jnp.concatenate([whole, part], 0).astype(BF16)


def in_order(odd_ref, own_ref, other_ref, out_ref):
    own, other = own_ref[...].astype(F32), other_ref[...].astype(F32)
    even = odd_ref[0] == 0
    first, second = jnp.where(even, own, other), jnp.where(even, other, own)
    out_ref[...] = jnp.concatenate([first, second], 0).astype(BF16)


def field(x_ref, y_ref, z_ref, coefficients_ref, conductivity_ref):
    wide_y = y_ref[...].astype(F32)
    scaled = x_ref[...].astype(F32) * coefficients_ref[...]
    left = [(scaled * wide_y[y : y + 1]).astype(BF16) for y in range(wide_y.shape[0])]
    logs = jnp.dot(jnp.concatenate(left, 0), z_ref[...], preferred_element_type=F32)
    conductivity_ref[...] = jnp.exp(logs)


def interpolation(
    meet, plane, cells_ref, chip_ref, arrived_ref, y_ref, z_ref, conductivity_ref,
    coefficients_ref, inverse_ref, near_eim_ref, far_eim_ref, turned_ref, kept_ref, error_ref,
    pick_x, pick_y, pick_z, wide_y,
):
    points, modes = pick_x.shape
    slabs = arrived_ref.shape[0]
    snaps = coefficients_ref.shape[0]
    width_z = conductivity_ref.shape[1]
    gram_width = arrived_ref.shape[2] - modes
    wide_y[...] = y_ref[...].astype(F32)
    lanes = lax.broadcasted_iota(jnp.int32, (1, width_z), 1)
    for q in range(points):
        cell = cells_ref[q]
        slab = (cell // plane + slabs - meet) % slabs
        pick_x[q : q + 1] = arrived_ref[slab][:, gram_width:].astype(F32)[1:2]
        pick_y[q : q + 1] = wide_y[pl.ds((cell % plane) // width_z, 1), :]
        pick_z[q : q + 1] = jnp.where(lanes == cell % width_z, 1.0, 0.0)
    at_z = lax.dot_general(
        pick_z[...].astype(BF16), z_ref[...], (((1,), (1,)), ((), ())), preferred_element_type=F32
    )
    at_x, at_y = pick_x[...], pick_y[...]
    coefficients = coefficients_ref[...]
    lane = lax.broadcasted_iota(jnp.int32, (points, 128), 1)
    logs = jnp.zeros((points, 128), F32)
    for s in range(snaps):
        left = ((at_x * coefficients[s : s + 1]) * at_y).astype(BF16).astype(F32)
        logs += jnp.where(lane == s, jnp.sum(left * at_z, axis=1, keepdims=True), 0.0)
    samples = jnp.exp(logs)
    values = jnp.dot(inverse_ref[...], samples, precision=EXACT, preferred_element_type=F32)
    turned = values.T[:snaps]
    turned_ref[...] = turned
    kept_ref[...] = turned
    depth = near_eim_ref.shape[0]
    swapped = jnp.concatenate([turned[:, depth:], turned[:, :depth]], 1)
    rounded = jnp.where(chip_ref[0] // 2 == 0, turned, swapped).astype(BF16)
    basis = jnp.concatenate([near_eim_ref[...], far_eim_ref[...]], 0)
    fitted = jnp.dot(rounded, basis, preferred_element_type=F32)
    for y in range(plane // width_z):
        part = slice(y * width_z, (y + 1) * width_z)
        error = conductivity_ref[y * snaps : (y + 1) * snaps] - fitted[:, part]
        error_ref[:, part] = error.astype(BF16)


def own_share(rank, odd_ref, arrived_ref, spread_ref):
    terms = spread_ref.shape[1]
    width = terms * rank
    half = rank // 2
    total = jnp.sum(arrived_ref[:, :, :width].astype(F32), axis=0)
    whole, part = total[0:1], total[1:2, : width // 2]
    odd = odd_ref[0] == 1
    picked = []
    for q in range(terms):
        first = whole[:, q * half : (q + 1) * half]
        second = whole[:, width // 2 + q * half : width // 2 + (q + 1) * half]
        single = part[:, q * half : (q + 1) * half]
        even_form = jnp.concatenate([first, second, single], 1)
        odd_form = jnp.concatenate([single, first, second], 1)
        picked.append(jnp.where(odd, odd_form, even_form))
    own = jnp.concatenate(picked, 0)
    for t in range(spread_ref.shape[0]):
        spread_ref[t] = own


def assembly(turn, core_ref, chip_ref, turned_ref, operators_ref, own_ref, out_ref):
    turned = turned_ref[...]
    count, terms = operators_ref.shape[:2]
    total = jnp.zeros(out_ref.shape, F32)
    for chip in range(count // 2):
        at = (2 * chip + count - turn) % count
        block = operators_ref[at] + operators_ref[at + 1]
        for j in range(terms):
            q = chip * terms + j
            total += turned[:, q : q + 1] * block[j : j + 1]
    out_ref[...] = total
    at = (2 * chip_ref[0] + count - turn) % count
    own = operators_ref[at] + operators_ref[at + 1]
    own_ref[...] = jnp.where(core_ref[0] == 0, own[: terms // 2], own[terms // 2 :])


def local(x_modes, y_modes, z_modes, coefficients, magic_cells, interp_inverse, eim_basis, basis):
    space, term = "space", "term"
    slabs, groups = lax.axis_size(space), lax.axis_size(term)
    modes = x_modes.shape[1]
    width_y, width_z = y_modes.shape[0], z_modes.shape[1]
    snaps, points = coefficients.shape[0], magic_cells.shape[0]
    rank, cells = basis.shape
    terms = eim_basis.shape[0]
    share = rank * rank // slabs
    shape = jax.ShapeDtypeStruct

    slab = lax.axis_index(space).astype(jnp.int32).reshape(1)
    place = lax.axis_index(term).astype(jnp.int32).reshape(1)
    core, chip = place % 2, place // 2
    side = chip % 2
    half = cells // 2
    meet, turn = slabs // 2 + slabs // 16, groups // 2
    ranks = [(meet + i) % slabs for i in range(slabs)]
    term_ranks = [(turn + i) % groups for i in range(groups)]
    swap = [(i, i ^ 1) for i in range(groups)]
    mine = pl.pallas_call(
        own_half,
        out_shape=shape((rank, half), BF16),
        grid_spec=pltpu.PrefetchScalarGridSpec(
            num_scalar_prefetch=1,
            grid=(1,),
            in_specs=[pl.BlockSpec((rank, half), lambda i, side_ref: (0, side_ref[0]))],
            out_specs=pl.BlockSpec((rank, half), lambda i, side_ref: (0, 0)),
        ),
        compiler_params=pltpu.CompilerParams(vmem_limit_bytes=32 << 20),
        cost_estimate=pl.CostEstimate(flops=0, bytes_accessed=2 * basis.size, transcendentals=0),
    )(core, basis)
    near = lax.ppermute(mine, space, [(i + 1, i) for i in range(slabs - 1)])
    eim_other = lax.ppermute(eim_basis, term, swap)
    gram_flops = 2 * rank * rank * terms * cells
    inner = call(
        lambda *refs: inner_gram(width_z, *refs),
        shape((terms * rank, rank), F32),
        (basis, eim_basis),
        flops=2 * gram_flops,
        moved=2 * basis.size,
    )
    eim_other, inner = lax.optimization_barrier((eim_other, inner))
    eim_pair = call(
        in_order,
        shape((2 * terms, cells), BF16),
        (core, eim_basis, eim_other),
        specs=[SMEM, VMEM, VMEM],
        moved=8 * eim_basis.size,
    )
    eim_beside = lax.ppermute(eim_pair, term, [(i, i ^ 2) for i in range(groups)])
    near, inner, eim_pair = lax.optimization_barrier((near, inner, eim_pair))
    packed = call(
        lambda *refs: outer_gram(ranks, *refs),
        shape((slabs, 2, terms * rank + modes), BF16),
        (core, basis, near, eim_pair, inner, x_modes),
        specs=[SMEM] + [VMEM] * 5,
        flops=gram_flops,
        moved=4 * basis.size,
    )
    packed, eim_beside, factors = lax.optimization_barrier((packed, eim_beside, coefficients))
    eim_near = call(
        in_order,
        shape((4 * terms, cells), BF16),
        (side, eim_pair, eim_beside),
        specs=[SMEM, VMEM, VMEM],
        moved=16 * eim_basis.size,
    )
    eim_far = lax.ppermute(eim_near, term, [(i, i ^ (groups - 2)) for i in range(groups)])
    arrived = lax.all_to_all(packed, space, 0, 0, axis_index_groups=[ranks], tiled=True)
    conductivity = call(
        field,
        shape((width_y * snaps, width_z), F32),
        (x_modes, y_modes, z_modes, factors),
        flops=2 * snaps * width_y * modes * width_z,
        moved=4 * points * cells,
    )
    arrived, conductivity = lax.optimization_barrier((arrived, conductivity))
    eim_turned, turned, interp_error = call(
        lambda *refs: interpolation(meet, cells, *refs),
        (shape((snaps, points), F32), shape((snaps, points), F32), shape((snaps, cells), BF16)),
        (magic_cells, chip, arrived, y_modes, z_modes, conductivity, coefficients, interp_inverse)
        + (eim_near, eim_far),
        specs=[SMEM] * 2 + [VMEM] * 8,
        scratch=[
            pltpu.VMEM((points, modes), F32),
            pltpu.VMEM((points, modes), F32),
            pltpu.VMEM((points, width_z), F32),
            pltpu.VMEM((width_y, modes), F32),
        ],
        flops=2 * snaps * points * cells,
        moved=4 * points * cells,
    )
    odd = slab % 2
    spread = call(
        lambda *refs: own_share(rank, *refs),
        shape((groups, 2 * terms, share), F32),
        (odd, arrived),
        specs=[SMEM, VMEM],
        moved=4 * packed.size,
    )
    all_operators = lax.all_to_all(spread, term, 0, 0, axis_index_groups=[term_ranks], tiled=True)
    term_operators, assembled = call(
        lambda *refs: assembly(turn, *refs),
        (shape((terms, share), F32), shape((snaps, share), F32)),
        (core, chip, turned, all_operators),
        specs=[SMEM, SMEM, VMEM, VMEM],
        moved=1 << 15,
    )
    return (eim_turned.T, interp_error, term_operators, assembled)


def solution(mesh):
    space, term = "space", "term"
    placed = (
        P(space, None),
        P(),
        P(),
        P(term, None),
        P(),
        P(),
        P(term, space),
        P(None, space),
    )
    return jax.shard_map(
        local,
        mesh=mesh,
        in_specs=placed,
        out_specs=(P(None, term), P(term, space), P(term, space), P(term, space)),
        check_vma=False,
    )
```
